32 devices in a mesh: section: 4 (over y, x), tp: 2 (over core), dp: 4 (over z).
Axes of the slice: x: 2, y: 2, z: 4, core: 2. Of those that a mesh axis runs over, the one named last changes fastest.
Arguments:
- hidden_states: bfloat16 [672, 8192], P(None, 'dp'), may hold values from -120 to 120
- norm_gain: float32 [8192], P('dp'), may hold values from 0.5 to 1.5
- lm_head: bfloat16 [8192, 19008], P('dp', ('section', 'tp')), may hold values from -6 to 6
- target_ids: int32 [672], replicated, may hold values from 0 to 19007
Outputs:
- logprobs: bfloat16 [672, 19008], P(None, ('section', 'tp', 'dp'))
- target_logprob: float32 [672], P('dp')
The draws below stay inside these ranges and needn't reach their ends.
All inputs are finite; a program needn't handle non-finite values.
Results may differ from the reference program's by a relative error of at most 0.0031.
Values may be sent and summed in bfloat16 or wider, within the bound.
A program may use at most 128 MiB of HBM per device.

```python
import math
import jax
import jax.numpy as jnp
import numpy as np
from jax import lax

D = 8192
ROWS = 672
VOCAB = 19008


def draw_hidden_states(key, part):
    key = jax.random.fold_in(key, 5)
    k_base, k_col, k_row = jax.random.split(key, 3)
    position = jnp.arange(D, dtype=jnp.float32) / D
    column = jnp.exp(0.55 * position) * jax.random.uniform(k_col, (D,), jnp.float32, 0.5, 1.5)
    row_scale = jnp.exp(jax.random.uniform(k_row, (ROWS, 1), jnp.float32, 0.0, 2.3))
    values = jax.random.truncated_normal(k_base, -4.0, 4.0, (ROWS, D), jnp.float32)
    return (values * column[None, :] * row_scale).astype(jnp.bfloat16)


def draw_lm_head(key, part):
    key = jax.random.fold_in(key, 9)
    k_base, k_col = jax.random.split(key, 2)
    position = jnp.arange(VOCAB, dtype=jnp.float32) / VOCAB
    column = 3.2 * (1.0 + 0.15 * position) * jax.random.uniform(k_col, (VOCAB,), jnp.float32, 0.6, 1.3)
    values = jax.random.truncated_normal(k_base, -4.0, 4.0, (D, VOCAB), jnp.float32) * column[None, :] / math.sqrt(D)
    return values.astype(jnp.bfloat16)


def with_ends(result, key, low, largest):
    longest = result.shape.index(max(result.shape))
    spots = []
    for shift in (0, 1):
        where = [jax.random.randint(jax.random.fold_in(key, axis), (), 0, length) for axis, length in enumerate(result.shape)]
        where[longest] = (where[longest] + shift) % result.shape[longest]
        spots.append(tuple(where))
    return result.at[spots[0]].set(low).at[spots[1]].set(largest)


def rank_table(count, slope):
    loads = [(1 << 20) // math.isqrt(rank ** slope) + 1 for rank in range(1, count + 1)]
    spread = 1 + sum(loads) // (1 << 30)
    return np.cumsum(np.array([max(1, weight // spread) for weight in loads]))


def skewed_ids(stream_key, dims, number_of, lean):
    table = rank_table(number_of, lean)
    ticket = jax.random.randint(jax.random.fold_in(stream_key, 1), dims, 0, int(table[number_of - 1]))
    standing = jnp.searchsorted(jnp.asarray(table, jnp.int32), ticket, side="right")
    return jax.random.permutation(jax.random.fold_in(stream_key, 2), number_of)[standing].astype(jnp.int32)


def setup_inputs(seed: int = 0) -> dict:
    splits = jax.random.split(jax.random.key(seed), 5)
    return {
        "hidden_states": draw_hidden_states(jax.random.fold_in(splits[4], 71), 0),
        "norm_gain": jnp.clip(1.0 + 0.1 * jax.random.normal(splits[1], (D,), jnp.float32), 0.5, 1.5),
        "lm_head": draw_lm_head(jax.random.fold_in(splits[4], 71), 0),
        "target_ids": with_ends(skewed_ids(splits[3], (ROWS,), VOCAB, 2), jax.random.fold_in(splits[3], 3), 0, VOCAB - 1).astype(jnp.int32),
    }


def reference(hidden_states, norm_gain, lm_head, target_ids):
    widened = hidden_states.astype(jnp.float32)
    mean_square = lax.optimization_barrier(jnp.mean(widened * widened, axis=1, keepdims=True))
    normed = (widened * lax.rsqrt(mean_square + 1e-06) * norm_gain[None, :]).astype(jnp.bfloat16)
    logits = jnp.dot(normed, lm_head, preferred_element_type=jnp.float32)
    row_top = lax.optimization_barrier(jnp.max(logits, axis=1, keepdims=True))
    row_total = lax.optimization_barrier(jnp.sum(jnp.exp(logits - row_top), axis=1, keepdims=True))
    logprobs = (logits - row_top - jnp.log(row_total)).astype(jnp.bfloat16)
    picked = jnp.take_along_axis(logits, target_ids.astype(jnp.int32)[:, None], axis=1)[:, 0]
    target_logprob = picked - row_top[:, 0] - jnp.log(row_total[:, 0])
    return (logprobs, target_logprob)
```

```python
import functools

import jax
import jax.numpy as jnp
from jax import lax
from jax.experimental import pallas as pl
from jax.experimental.pallas import tpu as pltpu
from jax.sharding import PartitionSpec as P

D = 8192

epsilon = 1e-06

MESH = pl.DeviceIdType.MESH
CHUNKS = 3
LANES = 128


def to_column(row):
    return jnp.broadcast_to(row, (LANES, row.shape[1])).T[:, :1]


def stack_rows(rows):
    place = lax.broadcasted_iota(jnp.int32, (8, rows[0].shape[1]), 0)
    result = jnp.zeros(place.shape, jnp.float32)
    for index, row in enumerate(rows):
        result = jnp.where(place == index, row, result)
    return result


def columns_to_rows(columns):
    place = lax.broadcasted_iota(jnp.int32, (columns[0].shape[0], LANES), 1)
    result = jnp.zeros(place.shape, jnp.float32)
    for index, column in enumerate(columns):
        result = jnp.where(place == index, column, result)
    return result.T[:8]


def merge(stats):
    tops, totals, picked = stats[:, 0:1], stats[:, 1:2], stats[:, 2:3]
    top = jnp.max(tops, axis=0)
    total = jnp.sum(totals * jnp.exp(tops - top[None]), axis=0)
    return top, total, jnp.sum(picked, axis=0)


def kernel(
    n, tp_size, plane, width, window, grain,
    x_hbm, w_hbm, gain_ref, target_ref,
    out_ref, target_out_ref,
    x_buf, w_buf, xg, part, send_buf, from_left, from_right, final, target_col,
    squares, all_squares, own_stats, plane_stats, own_merged, line_stats,
    load_sem, send_sem, left_sem, right_sem,
    sq_send, sq_recv, st_send, st_recv, ln_send, ln_recv,
):
    z = lax.axis_index("dp")
    me = lax.axis_index("section") * tp_size + lax.axis_index("tp")
    rc = xg.shape[1]

    load_x = pltpu.make_async_copy(x_hbm, x_buf, load_sem.at[0])
    load_w = pltpu.make_async_copy(w_hbm, w_buf, load_sem.at[1])
    load_x.start()
    load_w.start()

    def plane_peer(step):
        q = lax.rem(me + step, plane)
        return q, {"section": q // tp_size, "tp": lax.rem(q, tp_size)}

    def line_peer(step):
        q = lax.rem(z + step, n)
        return q, {"dp": q}

    barrier = pltpu.get_barrier_semaphore()

    def greet(peer, step, carry):
        pl.semaphore_signal(barrier, inc=1, device_id=peer(step)[1], device_id_type=MESH)
        return carry

    lax.fori_loop(1, plane, functools.partial(greet, plane_peer), 0)
    lax.fori_loop(1, n, functools.partial(greet, line_peer), 0)

    load_x.wait()
    gain = gain_ref[...]

    def prepare(r, carry):
        x = x_buf[pl.ds(pl.multiple_of(r * rc, 16), rc), :].astype(jnp.float32)
        xg[r] = (x * gain).astype(jnp.bfloat16)
        squares[r] = columns_to_rows([jnp.sum(x * x, axis=1, keepdims=True)])
        return carry

    lax.fori_loop(0, CHUNKS, prepare, 0)
    target_col[...] = jnp.broadcast_to(target_ref[...], (LANES, target_ref.shape[1])).T

    pl.semaphore_wait(barrier, plane - 1 + n - 1)

    def squares_copy(step, arriving):
        q, where = line_peer(step)
        return pltpu.make_async_remote_copy(
            src_ref=squares, dst_ref=all_squares.at[q if arriving else z],
            send_sem=sq_send.at[step], recv_sem=sq_recv.at[q if arriving else z],
            device_id=where, device_id_type=MESH,
        )

    def stats_copy(r, step, arriving):
        q, where = plane_peer(step)
        slot = q if arriving else me
        return pltpu.make_async_remote_copy(
            src_ref=own_stats.at[r], dst_ref=plane_stats.at[r, slot],
            send_sem=st_send.at[r, step], recv_sem=st_recv.at[r, slot],
            device_id=where, device_id_type=MESH,
        )

    def line_copy(r, step, arriving):
        q, where = line_peer(step)
        slot = q if arriving else z
        return pltpu.make_async_remote_copy(
            src_ref=own_merged.at[r], dst_ref=line_stats.at[r, slot],
            send_sem=ln_send.at[r, step], recv_sem=ln_recv.at[r, slot],
            device_id=where, device_id_type=MESH,
        )

    def each(first, last, action):
        def step_body(step, carry):
            action(step)
            return carry
        lax.fori_loop(first, last, step_body, 0)

    each(1, n, lambda step: squares_copy(step, False).start())
    all_squares[z] = squares[...]

    def right_copy(b, r):
        return pltpu.make_async_remote_copy(
            src_ref=send_buf.at[b, r], dst_ref=from_left.at[b, r],
            send_sem=send_sem.at[b, r], recv_sem=left_sem.at[b, r],
            device_id={"dp": lax.min(z + 1, n - 1)}, device_id_type=MESH,
        )

    def left_copy(b, r):
        return pltpu.make_async_remote_copy(
            src_ref=send_buf.at[b, r], dst_ref=from_right.at[b, r],
            send_sem=send_sem.at[b, r], recv_sem=right_sem.at[b, r],
            device_id={"dp": lax.max(z - 1, 0)}, device_id_type=MESH,
        )

    load_w.wait()

    def multiply(t, carry):
        r, i = t // n, lax.rem(t, n)
        b = jnp.where(z < n // 2, n - 1 - i, i)
        start = pl.multiple_of(width * b // grain * grain, grain)
        product = lax.dot_general(
            xg[r], w_buf[pl.ds(start, window), :],
            (((1,), (1,)), ((), ())), preferred_element_type=jnp.float32,
        )
        part[b, r] = product

        @pl.when((z == 0) & (b > 0))
        def _():
            send_buf[b, r] = product.astype(jnp.bfloat16)
            right_copy(b, r).start()

        @pl.when((z == n - 1) & (b < n - 1))
        def _():
            send_buf[b, r] = product.astype(jnp.bfloat16)
            left_copy(b, r).start()

        return carry

    lax.fori_loop(0, CHUNKS * n, multiply, 0)

    def forward(r, s):
        @pl.when((z >= 1) & (s >= z))
        def _():
            b = lax.min(n - 1 - s + z, n - 1)
            right_copy(b, r).wait_recv()
            send_buf[b, r] = (part[b, r] + from_left[b, r].astype(jnp.float32)).astype(jnp.bfloat16)
            right_copy(b, r).start()

        @pl.when((z <= n - 2) & (s >= n - 1 - z))
        def _():
            b = lax.max(s - (n - 1 - z), 0)
            left_copy(b, r).wait_recv()
            send_buf[b, r] = (part[b, r] + from_right[b, r].astype(jnp.float32)).astype(jnp.bfloat16)
            left_copy(b, r).start()

    padded = final.shape[2]

    def finish_sum(r):
        @pl.when(z >= 1)
        def _():
            right_copy(z, r).wait_recv()
            part[z, r] += from_left[z, r].astype(jnp.float32)

        @pl.when(z <= n - 2)
        def _():
            left_copy(z, r).wait_recv()
            part[z, r] += from_right[z, r].astype(jnp.float32)

        if r == 0:
            each(1, n, lambda step: squares_copy(step, True).wait_recv())
        total = jnp.sum(all_squares[:, r], axis=0)[0:1]
        scale = to_column(lax.rsqrt(total / D + epsilon))
        final[r, :, 0:window] = part[z, r] * scale
        moved = pltpu.roll(final[r], padded - (width * z - width * z // grain * grain), 1)
        final[r] = moved
        column = lax.broadcasted_iota(jnp.int32, moved.shape, 1)
        inside = column < width
        top = jnp.max(jnp.where(inside, moved, -jnp.inf), axis=1, keepdims=True)
        sum_exp = jnp.sum(jnp.where(inside, jnp.exp(moved - top), 0.0), axis=1, keepdims=True)
        wanted = target_col[r * rc:(r + 1) * rc, 0:1] - (me * n + z) * width
        hit = inside & (column == wanted)
        picked = jnp.sum(jnp.where(hit, moved, 0.0), axis=1, keepdims=True)
        stats = columns_to_rows([top, sum_exp, picked])
        own_stats[r] = stats
        plane_stats[r, me] = stats
        each(1, plane, lambda step: stats_copy(r, step, False).start())

    def merge_plane(r):
        each(1, plane, lambda step: stats_copy(r, step, True).wait_recv())
        merged = stack_rows(merge(plane_stats[r]))
        own_merged[r] = merged
        line_stats[r, z] = merged
        each(1, n, lambda step: line_copy(r, step, False).start())

    def emit(r):
        each(1, n, lambda step: line_copy(r, step, True).wait_recv())
        top, total, picked = merge(line_stats[r])
        norm = top + jnp.log(total)
        target_out_ref[r] = jnp.broadcast_to(picked - top - jnp.log(total), (8, rc))
        logprobs = final[r] - to_column(norm)
        out_ref[r * rc:(r + 1) * rc, :] = logprobs[:, :width].astype(jnp.bfloat16)

    final[...] = jnp.zeros(final.shape, jnp.float32)
    for r in range(CHUNKS):
        for s in range(1, n - 1):
            forward(r, s)
            if s == 1 and r >= 1:
                merge_plane(r - 1)
        if n == 2 and r >= 1:
            merge_plane(r - 1)
        if r >= 2:
            emit(r - 2)
        finish_sum(r)
    merge_plane(CHUNKS - 1)
    if CHUNKS >= 2:
        emit(CHUNKS - 2)
    emit(CHUNKS - 1)

    each(1, n, lambda step: squares_copy(step, False).wait_send())
    for r in range(CHUNKS):
        each(1, plane, lambda step: stats_copy(r, step, False).wait_send())
        each(1, n, lambda step: line_copy(r, step, False).wait_send())
        for b in range(n):
            @pl.when(b != z)
            def _():
                right_copy(b, r).wait_send()


def body(hidden_states, norm_gain, lm_head, target_ids):
    rows, depth = hidden_states.shape
    block = lm_head.shape[1]
    n, tp_size = lax.axis_size("dp"), lax.axis_size("tp")
    plane = lax.axis_size("section") * tp_size
    width = block // n
    grain = 16
    window = max(b * width % grain for b in range(n)) + width
    window = -(-window // 8) * 8
    assert (n - 1) * width // grain * grain + window <= block
    padded = -(-window // LANES) * LANES
    rc = rows // CHUNKS
    f32, bf16 = jnp.float32, jnp.bfloat16
    any_space = pl.BlockSpec(memory_space=pl.ANY)
    vmem = pl.BlockSpec(memory_space=pltpu.VMEM)
    dma = pltpu.SemaphoreType.DMA
    logprobs, target = pl.pallas_call(
        functools.partial(kernel, n, tp_size, plane, width, window, grain),
        out_shape=(
            jax.ShapeDtypeStruct((rows, width), bf16),
            jax.ShapeDtypeStruct((CHUNKS, 8, rc), f32),
        ),
        in_specs=[any_space, any_space, vmem, vmem],
        out_specs=(vmem, vmem),
        scratch_shapes=[
            pltpu.VMEM((rows, depth), bf16),
            pltpu.VMEM((block, depth), bf16),
            pltpu.VMEM((CHUNKS, rc, depth), bf16),
            pltpu.VMEM((n, CHUNKS, rc, window), f32),
            pltpu.VMEM((n, CHUNKS, rc, window), bf16),
            pltpu.VMEM((n, CHUNKS, rc, window), bf16),
            pltpu.VMEM((n, CHUNKS, rc, window), bf16),
            pltpu.VMEM((CHUNKS, rc, padded), f32),
            pltpu.VMEM((rows, LANES), jnp.int32),
            pltpu.VMEM((CHUNKS, 8, rc), f32),
            pltpu.VMEM((n, CHUNKS, 8, rc), f32),
            pltpu.VMEM((CHUNKS, 8, rc), f32),
            pltpu.VMEM((CHUNKS, plane, 8, rc), f32),
            pltpu.VMEM((CHUNKS, 8, rc), f32),
            pltpu.VMEM((CHUNKS, n, 8, rc), f32),
            dma((2,)),
            dma((n, CHUNKS)),
            dma((n, CHUNKS)),
            dma((n, CHUNKS)),
            dma((n,)),
            dma((n,)),
            dma((CHUNKS, plane)),
            dma((CHUNKS, plane)),
            dma((CHUNKS, n)),
            dma((CHUNKS, n)),
        ],
        compiler_params=pltpu.CompilerParams(
            collective_id=0, has_side_effects=True, vmem_limit_bytes=56 * 1024 * 1024
        ),
        cost_estimate=pl.CostEstimate(
            flops=2 * rows * depth * block,
            bytes_accessed=2 * (rows * depth + depth * block + rows * width),
            transcendentals=rows * width,
        ),
    )(hidden_states, lm_head.T, norm_gain[None, :], target_ids[None, :])
    own_rows = rows // n
    target = target[:, 0, :].reshape(rows)
    return logprobs, lax.dynamic_slice_in_dim(target, lax.axis_index("dp") * own_rows, own_rows, 0)


def solution(mesh):
    placed = (P(None, "dp"), P("dp"), P("dp", ("section", "tp")), P())
    return jax.shard_map(
        body,
        mesh=mesh,
        in_specs=placed,
        out_specs=(P(None, ("section", "tp", "dp")), P("dp")),
        check_vma=False,
    )
```

```python
import functools

import jax
import jax.numpy as jnp
from jax import lax
from jax.experimental import pallas as pl
from jax.experimental.pallas import tpu as pltpu
from jax.sharding import PartitionSpec as P

D = 8192

epsilon = 1e-06

MESH = pl.DeviceIdType.MESH
CHUNKS = 7
LANES = 128
GRAIN = 16


def to_column(row):
    return jnp.broadcast_to(row, (LANES, row.shape[1])).T[:, :1]


def stack_rows(rows):
    place = lax.broadcasted_iota(jnp.int32, (8, rows[0].shape[1]), 0)
    result = jnp.zeros(place.shape, jnp.float32)
    for index, row in enumerate(rows):
        result = jnp.where(place == index, row, result)
    return result


def columns_to_rows(columns):
    place = lax.broadcasted_iota(jnp.int32, (columns[0].shape[0], LANES), 1)
    result = jnp.zeros(place.shape, jnp.float32)
    for index, column in enumerate(columns):
        result = jnp.where(place == index, column, result)
    return result.T[:8]


def merge(stats):
    tops, totals, picked = stats[:, 0:1], stats[:, 1:2], stats[:, 2:3]
    top = jnp.max(tops, axis=0)
    total = jnp.sum(totals * jnp.exp(tops - top[None]), axis=0)
    return top, total, jnp.sum(picked, axis=0)


def plan(n, width, block):
    origin = width // GRAIN * GRAIN
    starts = [(width * b - origin) // LANES * LANES for b in range(1, n)] + [block - origin]
    right = [None] + [(origin + lo, hi - lo) for lo, hi in zip(starts, starts[1:])]
    ends = [0] + [-(-width * (b + 1) // LANES) * LANES for b in range(n - 1)]
    left = [(lo, hi - lo) for lo, hi in zip(ends, ends[1:])]
    own = []
    for b in range(n):
        first = width * b // GRAIN * GRAIN
        own.append((first, -(-(width * b - first + width) // 8) * 8))
    return right, left, own


def whole_tiles(count):
    return -(-count // LANES) * LANES


def kernel(
    n, tp_size, plane, width,
    x_hbm, w_hbm, gain_ref, target_ref,
    out_ref, target_out_ref,
    x_buf, w_buf, xg, part, own_part, final, target_col, target_row,
    squares, all_squares, own_stats, plane_stats, own_merged, line_stats,
    load_sem, send_sem, left_sem, right_sem,
    sq_send, sq_recv, st_send, st_recv, ln_send, ln_recv,
    *travel,
):
    z = lax.axis_index("dp")
    me = lax.axis_index("section") * tp_size + lax.axis_index("tp")
    rc = xg.shape[1]
    right, left, own = plan(n, width, w_buf.shape[0])
    send_right, travel = (None,) + travel[:n - 1], travel[n - 1:]
    from_left, travel = (None,) + travel[:n - 1], travel[n - 1:]
    send_left, from_right = travel[:n - 1], travel[n - 1:]

    load_x = pltpu.make_async_copy(x_hbm, x_buf, load_sem.at[0])
    load_w = pltpu.make_async_copy(w_hbm, w_buf, load_sem.at[1])
    load_x.start()
    load_w.start()

    def plane_peer(step):
        q = lax.rem(me + step, plane)
        return q, {"section": q // tp_size, "tp": lax.rem(q, tp_size)}

    def line_peer(step):
        q = lax.rem(z + step, n)
        return q, {"dp": q}

    barrier = pltpu.get_barrier_semaphore()

    def greet(peer, step, carry):
        pl.semaphore_signal(barrier, inc=1, device_id=peer(step)[1], device_id_type=MESH)
        return carry

    lax.fori_loop(1, plane, functools.partial(greet, plane_peer), 0)
    lax.fori_loop(1, n, functools.partial(greet, line_peer), 0)

    target_col[...] = jnp.broadcast_to(
        target_ref[...].reshape(1, target_ref.shape[0]), (LANES, target_ref.shape[0])
    ).T
    load_x.wait()
    gain = gain_ref[...]

    def prepare(r, carry):
        x = x_buf[pl.ds(pl.multiple_of(r * rc, 16), rc), :].astype(jnp.float32)
        xg[r] = (x * gain).astype(jnp.bfloat16)
        squares[r] = columns_to_rows([jnp.sum(x * x, axis=1, keepdims=True)])
        return carry

    lax.fori_loop(0, CHUNKS, prepare, 0)
    pl.semaphore_wait(barrier, plane - 1 + n - 1)

    def squares_copy(step, arriving):
        q, where = line_peer(step)
        slot = q if arriving else z
        return pltpu.make_async_remote_copy(
            src_ref=squares, dst_ref=all_squares.at[slot],
            send_sem=sq_send.at[step], recv_sem=sq_recv.at[slot],
            device_id=where, device_id_type=MESH,
        )

    def stats_copy(r, step, arriving):
        q, where = plane_peer(step)
        slot = q if arriving else me
        return pltpu.make_async_remote_copy(
            src_ref=own_stats.at[r], dst_ref=plane_stats.at[r, slot],
            send_sem=st_send.at[r, step], recv_sem=st_recv.at[r, slot],
            device_id=where, device_id_type=MESH,
        )

    def line_copy(r, step, arriving):
        q, where = line_peer(step)
        slot = q if arriving else z
        return pltpu.make_async_remote_copy(
            src_ref=own_merged.at[r], dst_ref=line_stats.at[r, slot],
            send_sem=ln_send.at[r, step], recv_sem=ln_recv.at[r, slot],
            device_id=where, device_id_type=MESH,
        )

    def each(first, last, action):
        def step_body(step, carry):
            action(step)
            return carry
        lax.fori_loop(first, last, step_body, 0)

    each(1, n, lambda step: squares_copy(step, False).start())
    all_squares[z] = squares[...]
    load_w.wait()

    def right_copy(at, b, r):
        return pltpu.make_async_remote_copy(
            src_ref=send_right[b].at[r], dst_ref=from_left[b].at[r],
            send_sem=send_sem.at[b, r], recv_sem=left_sem.at[b, r],
            device_id={"dp": min(at + 1, n - 1)}, device_id_type=MESH,
        )

    def left_copy(at, b, r):
        return pltpu.make_async_remote_copy(
            src_ref=send_left[b].at[r], dst_ref=from_right[b].at[r],
            send_sem=send_sem.at[b, r], recv_sem=right_sem.at[b, r],
            device_id={"dp": max(at - 1, 0)}, device_id_type=MESH,
        )

    def product(r, piece):
        first, count = piece
        return lax.dot_general(
            xg[r], w_buf[first:first + count, :],
            (((1,), (1,)), ((), ())), preferred_element_type=jnp.float32,
        )

    def shifted(parts, lead):
        lanes = jnp.concatenate([p.astype(jnp.float32) for p in parts], axis=1) if len(parts) > 1 else parts[0].astype(jnp.float32)
        if lead:
            lanes = pltpu.roll(lanes, lanes.shape[1] - lead, 1)
        return lanes[:, :final.shape[2]]

    def window(buffers, pieces, origin, at, r):
        lo, hi = width * at, width * (at + 1)
        first, parts = None, []
        for buffer, piece in zip(buffers, pieces):
            if piece is None or piece[0] + piece[1] <= lo or piece[0] >= hi:
                continue
            begin = max(lo - piece[0], 0) // LANES * LANES
            end = min(whole_tiles(hi - piece[0]), whole_tiles(piece[1]))
            if first is None:
                first = piece[0] + begin
            parts.append(buffer[r, :, begin:end])
        return shifted(parts, lo - first)

    def run(at):
        going = [(at + n - 1 - b, "right", b) for b in range(n - 1, at, -1)]
        going += [(n - 1 - at + b, "left", b) for b in range(at)]
        going.sort(key=lambda entry: entry[0])

        def multiply(r):
            for _, way, b in going:
                piece = right[b] if way == "right" else left[b]
                result = product(r, piece)
                if way == "right" and at == 0:
                    send_right[b][r, :, :piece[1]] = result.astype(jnp.bfloat16)
                    right_copy(at, b, r).start()
                elif way == "left" and at == n - 1:
                    send_left[b][r, :, :piece[1]] = result.astype(jnp.bfloat16)
                    left_copy(at, b, r).start()
                else:
                    part[b, r, :, :piece[1]] = result
            own_part[r, :, :own[at][1]] = product(r, own[at])

        def forward(r):
            for _, way, b in going:
                if way == "right" and at > 0:
                    count = right[b][1]
                    right_copy(at, b, r).wait_recv()
                    send_right[b][r, :, :count] = (
                        part[b, r, :, :count] + from_left[b][r, :, :count].astype(jnp.float32)
                    ).astype(jnp.bfloat16)
                    right_copy(at, b, r).start()
                elif way == "left" and at < n - 1:
                    count = left[b][1]
                    left_copy(at, b, r).wait_recv()
                    send_left[b][r, :, :count] = (
                        part[b, r, :, :count] + from_right[b][r, :, :count].astype(jnp.float32)
                    ).astype(jnp.bfloat16)
                    left_copy(at, b, r).start()

        def finish_sum(r):
            total = jnp.sum(all_squares[:, r], axis=0)[0:1]
            scale = to_column(lax.rsqrt(total / D + epsilon))
            logits = shifted([own_part[r]], width * at - own[at][0])
            if at > 0:
                right_copy(at, at, r).wait_recv()
                logits += window(from_left, right, right[1][0], at, r)
            if at < n - 1:
                left_copy(at, at, r).wait_recv()
                logits += window(from_right, left, 0, at, r)
            logits *= scale
            final[r] = logits
            column = lax.broadcasted_iota(jnp.int32, logits.shape, 1)
            inside = column < width
            top = jnp.max(jnp.where(inside, logits, -jnp.inf), axis=1, keepdims=True)
            sum_exp = jnp.sum(jnp.where(inside, jnp.exp(logits - top), 0.0), axis=1, keepdims=True)
            wanted = target_col[pl.ds(pl.multiple_of(r * rc, 16), rc), 0:1] - (me * n + at) * width
            hit = inside & (column == wanted)
            picked = jnp.sum(jnp.where(hit, logits, 0.0), axis=1, keepdims=True)
            stats = columns_to_rows([top, sum_exp, picked])
            own_stats[r] = stats
            plane_stats[r, me] = stats
            each(1, plane, lambda step: stats_copy(r, step, False).start())

        def merge_plane(r):
            each(1, plane, lambda step: stats_copy(r, step, True).wait_recv())
            merged = stack_rows(merge(plane_stats[r]))
            own_merged[r] = merged
            line_stats[r, at] = merged
            each(1, n, lambda step: line_copy(r, step, False).start())

        def emit(r):
            each(1, n, lambda step: line_copy(r, step, True).wait_recv())
            top, total, picked = merge(line_stats[r])
            rest = jnp.log(total)
            target_row[r, :, :rc] = jnp.broadcast_to(picked - top - rest, (8, rc))
            logprobs = final[r] - to_column(top + rest)
            out_ref[pl.ds(pl.multiple_of(r * rc, 16), rc), :] = logprobs[:, :width].astype(jnp.bfloat16)

        multiply(0)
        each(1, n, lambda step: squares_copy(step, True).wait_recv())

        def chunk(r, carry):
            @pl.when(r + 1 < CHUNKS)
            def _():
                multiply(r + 1)
            forward(r)

            @pl.when(r >= 1)
            def _():
                merge_plane(r - 1)

            @pl.when(r >= 2)
            def _():
                emit(r - 2)
            finish_sum(r)
            return carry

        lax.fori_loop(0, CHUNKS, chunk, 0)
        merge_plane(CHUNKS - 1)
        emit(CHUNKS - 2)
        emit(CHUNKS - 1)

        own_rows = target_out_ref.shape[1]
        lo = own_rows * at
        lanes = target_row.shape[2]
        place = lax.broadcasted_iota(jnp.int32, (8, lanes), 1) + lo
        row = jnp.zeros((8, lanes), jnp.float32)
        for c in range(lo // rc, (lo + own_rows - 1) // rc + 1):
            moved = pltpu.roll(target_row[c], (c * rc - lo) % lanes, 1)
            row = jnp.where((place >= c * rc) & (place < (c + 1) * rc), moved, row)
        target_out_ref[...] = row[0:1, :own_rows]

        for r in range(CHUNKS):
            for _, way, b in going:
                (right_copy if way == "right" else left_copy)(at, b, r).wait_send()

    for at in range(n):
        pl.when(z == at)(functools.partial(run, at))

    each(1, n, lambda step: squares_copy(step, False).wait_send())

    def drain(r, carry):
        each(1, plane, lambda step: stats_copy(r, step, False).wait_send())
        each(1, n, lambda step: line_copy(r, step, False).wait_send())
        return carry

    lax.fori_loop(0, CHUNKS, drain, 0)


def body(hidden_states, norm_gain, lm_head, target_ids):
    rows, depth = hidden_states.shape
    block = lm_head.shape[1]
    n, tp_size = lax.axis_size("dp"), lax.axis_size("tp")
    plane = lax.axis_size("section") * tp_size
    width = block // n
    right, left, own = plan(n, width, block)
    widest = max(whole_tiles(piece[1]) for piece in right[1:] + left + own)
    rc = rows // CHUNKS
    own_rows = rows // n
    f32, bf16 = jnp.float32, jnp.bfloat16
    any_space = pl.BlockSpec(memory_space=pl.ANY)
    vmem = pl.BlockSpec(memory_space=pltpu.VMEM)
    dma = pltpu.SemaphoreType.DMA
    travel = [pltpu.VMEM((CHUNKS, rc, whole_tiles(piece[1])), bf16) for piece in right[1:] * 2 + left * 2]
    logprobs, target = pl.pallas_call(
        functools.partial(kernel, n, tp_size, plane, width),
        out_shape=(
            jax.ShapeDtypeStruct((rows, width), bf16),
            jax.ShapeDtypeStruct((1, own_rows), f32),
        ),
        in_specs=[any_space, any_space, vmem, vmem],
        out_specs=(vmem, vmem),
        scratch_shapes=[
            pltpu.VMEM((rows, depth), bf16),
            pltpu.VMEM((block, depth), bf16),
            pltpu.VMEM((CHUNKS, rc, depth), bf16),
            pltpu.VMEM((n, CHUNKS, rc, widest), f32),
            pltpu.VMEM((CHUNKS, rc, widest), f32),
            pltpu.VMEM((CHUNKS, rc, whole_tiles(width)), f32),
            pltpu.VMEM((rows, LANES), jnp.int32),
            pltpu.VMEM((CHUNKS, 8, whole_tiles(rc + own_rows)), f32),
            pltpu.VMEM((CHUNKS, 8, rc), f32),
            pltpu.VMEM((n, CHUNKS, 8, rc), f32),
            pltpu.VMEM((CHUNKS, 8, rc), f32),
            pltpu.VMEM((CHUNKS, plane, 8, rc), f32),
            pltpu.VMEM((CHUNKS, 8, rc), f32),
            pltpu.VMEM((CHUNKS, n, 8, rc), f32),
            dma((2,)),
            dma((n, CHUNKS)),
            dma((n, CHUNKS)),
            dma((n, CHUNKS)),
            dma((n,)),
            dma((n,)),
            dma((CHUNKS, plane)),
            dma((CHUNKS, plane)),
            dma((CHUNKS, n)),
            dma((CHUNKS, n)),
        ] + travel,
        compiler_params=pltpu.CompilerParams(
            collective_id=0, has_side_effects=True, vmem_limit_bytes=52 * 1024 * 1024
        ),
        cost_estimate=pl.CostEstimate(
            flops=2 * rows * depth * block,
            bytes_accessed=2 * (rows * depth + depth * block + rows * width),
            transcendentals=rows * width,
        ),
    )(hidden_states, lm_head.T, norm_gain[None, :], target_ids)
    return logprobs, target.reshape(own_rows)


def solution(mesh):
    placed = (P(None, "dp"), P("dp"), P("dp", ("section", "tp")), P())
    return jax.shard_map(
        body,
        mesh=mesh,
        in_specs=placed,
        out_specs=(P(None, ("section", "tp", "dp")), P("dp")),
        check_vma=False,
    )
```

```python
import functools

import jax
import jax.numpy as jnp
from jax import lax
from jax.experimental import pallas as pl
from jax.experimental.pallas import tpu as pltpu
from jax.sharding import PartitionSpec as P

D = 8192

epsilon = 1e-06

MESH = pl.DeviceIdType.MESH
CHUNKS = 7
LANES = 128
GRAIN = 8


def to_column(row):
    return jnp.broadcast_to(row, (LANES, row.shape[1])).T[:, :1]


def stack_rows(rows):
    place = lax.broadcasted_iota(jnp.int32, (8, rows[0].shape[1]), 0)
    result = jnp.zeros(place.shape, jnp.float32)
    for index, row in enumerate(rows):
        result = jnp.where(place == index, row, result)
    return result


def columns_to_rows(columns):
    place = lax.broadcasted_iota(jnp.int32, (columns[0].shape[0], LANES), 1)
    result = jnp.zeros(place.shape, jnp.float32)
    for index, column in enumerate(columns):
        result = jnp.where(place == index, column, result)
    return result.T[:8]


def merge(stats):
    tops, totals, picked = stats[:, 0:1], stats[:, 1:2], stats[:, 2:3]
    top = jnp.max(tops, axis=0)
    total = jnp.sum(totals * jnp.exp(tops - top[None]), axis=0)
    return top, total, jnp.sum(picked, axis=0)


def plan(n, width, block):
    origin = block - whole_tiles(block - width)
    starts = [(width * b - origin) // LANES * LANES for b in range(1, n)] + [block - origin]
    right = [None] + [(origin + lo, hi - lo) for lo, hi in zip(starts, starts[1:])]
    ends = [0] + [-(-width * (b + 1) // LANES) * LANES for b in range(n - 1)]
    left = [(lo, hi - lo) for lo, hi in zip(ends, ends[1:])]
    widest = max(piece[1] for piece in right[1:] + left)
    own = [(min(width * b // GRAIN * GRAIN, block - widest), widest) for b in range(n)]
    return right, left, own


def travel_order(n, at):
    going = [(at + n - 1 - b, "right", b) for b in range(n - 1, at, -1)]
    going += [(n - 1 - at + b, "left", b) for b in range(at)]
    return [entry[1:] for entry in sorted(going, key=lambda entry: entry[0])]


def whole_tiles(count):
    return -(-count // LANES) * LANES


def kernel(
    n, tp_size, plane, width,
    x_hbm, w_hbm, gain_ref, target_ref,
    out_ref, target_out_ref,
    x_buf, w_buf, xg, part, final, target_col, target_row,
    squares, all_squares, own_stats, plane_stats, own_merged, line_stats,
    load_sem, send_sem, left_sem, right_sem,
    sq_send, sq_recv, st_send, st_recv, ln_send, ln_recv,
    *travel,
):
    z = lax.axis_index("dp")
    me = lax.axis_index("section") * tp_size + lax.axis_index("tp")
    rc, widest = xg.shape[0] // CHUNKS, part.shape[2]
    right, left, own = plan(n, width, w_buf.shape[0])
    send_right, travel = (None,) + travel[:n - 1], travel[n - 1:]
    from_left, travel = (None,) + travel[:n - 1], travel[n - 1:]
    send_left, from_right = travel[:n - 1], travel[n - 1:]

    load_x = pltpu.make_async_copy(x_hbm, x_buf, load_sem.at[0])
    load_w = pltpu.make_async_copy(w_hbm, w_buf, load_sem.at[1])
    load_x.start()
    load_w.start()

    def plane_peer(step):
        q = lax.rem(me + step, plane)
        return q, {"section": q // tp_size, "tp": lax.rem(q, tp_size)}

    def line_peer(step):
        q = lax.rem(z + step, n)
        return q, {"dp": q}

    barrier = pltpu.get_barrier_semaphore()

    def greet(peer, step, carry):
        pl.semaphore_signal(barrier, inc=1, device_id=peer(step)[1], device_id_type=MESH)
        return carry

    lax.fori_loop(1, plane, functools.partial(greet, plane_peer), 0)
    lax.fori_loop(1, n, functools.partial(greet, line_peer), 0)

    target_col[...] = jnp.broadcast_to(
        target_ref[...].reshape(1, target_ref.shape[0]), (LANES, target_ref.shape[0])
    ).T
    load_x.wait()
    gain = gain_ref[...]

    def prepare(r, carry):
        x = x_buf[pl.ds(pl.multiple_of(r * rc, 16), rc), :].astype(jnp.float32)
        xg[pl.ds(pl.multiple_of(r * rc, 16), rc), :] = (x * gain).astype(jnp.bfloat16)
        squares[r] = columns_to_rows([jnp.sum(x * x, axis=1, keepdims=True)])
        return carry

    lax.fori_loop(0, CHUNKS, prepare, 0)
    pl.semaphore_wait(barrier, plane - 1 + n - 1)

    def squares_copy(step, arriving):
        q, where = line_peer(step)
        slot = q if arriving else z
        return pltpu.make_async_remote_copy(
            src_ref=squares, dst_ref=all_squares.at[slot],
            send_sem=sq_send.at[step], recv_sem=sq_recv.at[slot],
            device_id=where, device_id_type=MESH,
        )

    def stats_copy(r, step, arriving):
        q, where = plane_peer(step)
        slot = q if arriving else me
        return pltpu.make_async_remote_copy(
            src_ref=own_stats.at[r], dst_ref=plane_stats.at[r, slot],
            send_sem=st_send.at[r, step], recv_sem=st_recv.at[r, slot],
            device_id=where, device_id_type=MESH,
        )

    def line_copy(r, step, arriving):
        q, where = line_peer(step)
        slot = q if arriving else z
        return pltpu.make_async_remote_copy(
            src_ref=own_merged.at[r], dst_ref=line_stats.at[r, slot],
            send_sem=ln_send.at[r, step], recv_sem=ln_recv.at[r, slot],
            device_id=where, device_id_type=MESH,
        )

    def each(first, last, action):
        def step_body(step, carry):
            action(step)
            return carry
        lax.fori_loop(first, last, step_body, 0)

    each(1, n, lambda step: squares_copy(step, False).start())
    all_squares[z] = squares[...]
    load_w.wait()

    def right_copy(at, b, r):
        return pltpu.make_async_remote_copy(
            src_ref=send_right[b].at[r], dst_ref=from_left[b].at[r],
            send_sem=send_sem.at[b, r], recv_sem=left_sem.at[b, r],
            device_id={"dp": min(at + 1, n - 1)}, device_id_type=MESH,
        )

    def left_copy(at, b, r):
        return pltpu.make_async_remote_copy(
            src_ref=send_left[b].at[r], dst_ref=from_right[b].at[r],
            send_sem=send_sem.at[b, r], recv_sem=right_sem.at[b, r],
            device_id={"dp": max(at - 1, 0)}, device_id_type=MESH,
        )

    orders = [travel_order(n, at) for at in range(n)]

    def rows_of(r):
        return pl.ds(pl.multiple_of(r * rc, 16), rc)

    def start_own(at, k, r):
        way, b = orders[at][k]
        if way == "right":
            send_right[b][r] = part[k, rows_of(r), :right[b][1]].astype(jnp.bfloat16)
            right_copy(at, b, r).start()
        else:
            send_left[b][r] = part[k, rows_of(r), :left[b][1]].astype(jnp.bfloat16)
            left_copy(at, b, r).start()

    def multiply(k, carry):
        first = 0
        for at in range(n):
            pieces = [(right if way == "right" else left)[b] for way, b in orders[at]] + [own[at]]
            for index, piece in enumerate(pieces):
                first = jnp.where((z == at) & (k == index), piece[0], first)
        part[k] = lax.dot_general(
            xg[...], w_buf[pl.ds(pl.multiple_of(first, GRAIN), widest), :],
            (((1,), (1,)), ((), ())), preferred_element_type=jnp.float32,
        )
        for at in (0, n - 1):
            for index in range(n - 1):
                pl.when((z == at) & (k == index))(functools.partial(start_own, at, index, 0))
        return carry

    lax.fori_loop(0, n, multiply, 0)

    def shifted(parts, lead):
        lanes = jnp.concatenate([p.astype(jnp.float32) for p in parts], axis=1) if len(parts) > 1 else parts[0].astype(jnp.float32)
        if lead:
            lanes = pltpu.roll(lanes, lanes.shape[1] - lead, 1)
        return lanes[:, :final.shape[2]]

    def window(buffers, pieces, origin, at, r):
        lo, hi = width * at, width * (at + 1)
        first, parts = None, []
        for buffer, piece in zip(buffers, pieces):
            if piece is None or piece[0] + piece[1] <= lo or piece[0] >= hi:
                continue
            begin = max(lo - piece[0], 0) // LANES * LANES
            end = min(whole_tiles(hi - piece[0]), whole_tiles(piece[1]))
            if first is None:
                first = piece[0] + begin
            parts.append(buffer[r, :, begin:end])
        return shifted(parts, lo - first)

    def run(at):
        going = orders[at]
        end = at in (0, n - 1)

        def forward(r):
            for k, (way, b) in enumerate(going):
                if way == "right":
                    count = right[b][1]
                    right_copy(at, b, r).wait_recv()
                    send_right[b][r] = (
                        part[k, rows_of(r), :count] + from_left[b][r].astype(jnp.float32)
                    ).astype(jnp.bfloat16)
                    right_copy(at, b, r).start()
                else:
                    count = left[b][1]
                    left_copy(at, b, r).wait_recv()
                    send_left[b][r] = (
                        part[k, rows_of(r), :count] + from_right[b][r].astype(jnp.float32)
                    ).astype(jnp.bfloat16)
                    left_copy(at, b, r).start()

        def finish_sum(r):
            total = jnp.sum(all_squares[:, r], axis=0)[0:1]
            scale = to_column(lax.rsqrt(total / D + epsilon))
            logits = shifted([part[n - 1, rows_of(r)]], width * at - own[at][0])
            if at > 0:
                right_copy(at, at, r).wait_recv()
                logits += window(from_left, right, right[1][0], at, r)
            if at < n - 1:
                left_copy(at, at, r).wait_recv()
                logits += window(from_right, left, 0, at, r)
            logits *= scale
            final[r] = logits
            column = lax.broadcasted_iota(jnp.int32, logits.shape, 1)
            inside = column < width
            top = jnp.max(jnp.where(inside, logits, -jnp.inf), axis=1, keepdims=True)
            sum_exp = jnp.sum(jnp.where(inside, jnp.exp(logits - top), 0.0), axis=1, keepdims=True)
            wanted = target_col[pl.ds(pl.multiple_of(r * rc, 16), rc), 0:1] - (me * n + at) * width
            hit = inside & (column == wanted)
            picked = jnp.sum(jnp.where(hit, logits, 0.0), axis=1, keepdims=True)
            stats = columns_to_rows([top, sum_exp, picked])
            own_stats[r] = stats
            plane_stats[r, me] = stats
            each(1, plane, lambda step: stats_copy(r, step, False).start())

        def merge_plane(r):
            each(1, plane, lambda step: stats_copy(r, step, True).wait_recv())
            merged = stack_rows(merge(plane_stats[r]))
            own_merged[r] = merged
            line_stats[r, at] = merged
            each(1, n, lambda step: line_copy(r, step, False).start())

        def emit(r):
            each(1, n, lambda step: line_copy(r, step, True).wait_recv())
            top, total, picked = merge(line_stats[r])
            rest = jnp.log(total)
            target_row[r, :, :rc] = jnp.broadcast_to(picked - top - rest, (8, rc))
            logprobs = final[r] - to_column(top + rest)
            out_ref[pl.ds(pl.multiple_of(r * rc, 16), rc), :] = logprobs[:, :width].astype(jnp.bfloat16)

        each(1, n, lambda step: squares_copy(step, True).wait_recv())

        def chunk(r, carry):
            if end:
                @pl.when(r + 1 < CHUNKS)
                def _():
                    for k in range(n - 1):
                        start_own(at, k, r + 1)
            else:
                forward(r)

            @pl.when(r >= 1)
            def _():
                merge_plane(r - 1)

            @pl.when(r >= 2)
            def _():
                emit(r - 2)
            finish_sum(r)
            return carry

        lax.fori_loop(0, CHUNKS, chunk, 0)
        merge_plane(CHUNKS - 1)
        emit(CHUNKS - 2)
        emit(CHUNKS - 1)

        own_rows = target_out_ref.shape[1]
        lo = own_rows * at
        lanes = target_row.shape[2]
        place = lax.broadcasted_iota(jnp.int32, (8, lanes), 1) + lo
        row = jnp.zeros((8, lanes), jnp.float32)
        for c in range(lo // rc, (lo + own_rows - 1) // rc + 1):
            moved = pltpu.roll(target_row[c], (c * rc - lo) % lanes, 1)
            row = jnp.where((place >= c * rc) & (place < (c + 1) * rc), moved, row)
        target_out_ref[...] = row[0:1, :own_rows]

        for r in range(CHUNKS):
            for way, b in going:
                (right_copy if way == "right" else left_copy)(at, b, r).wait_send()

    for at in range(n):
        pl.when(z == at)(functools.partial(run, at))

    each(1, n, lambda step: squares_copy(step, False).wait_send())

    def drain(r, carry):
        each(1, plane, lambda step: stats_copy(r, step, False).wait_send())
        each(1, n, lambda step: line_copy(r, step, False).wait_send())
        return carry

    lax.fori_loop(0, CHUNKS, drain, 0)


def body(hidden_states, norm_gain, lm_head, target_ids):
    rows, depth = hidden_states.shape
    block = lm_head.shape[1]
    n, tp_size = lax.axis_size("dp"), lax.axis_size("tp")
    plane = lax.axis_size("section") * tp_size
    width = block // n
    right, left, own = plan(n, width, block)
    widest = max(whole_tiles(piece[1]) for piece in right[1:] + left + own)
    rc = rows // CHUNKS
    own_rows = rows // n
    f32, bf16 = jnp.float32, jnp.bfloat16
    any_space = pl.BlockSpec(memory_space=pl.ANY)
    vmem = pl.BlockSpec(memory_space=pltpu.VMEM)
    dma = pltpu.SemaphoreType.DMA
    travel = [pltpu.VMEM((CHUNKS, rc, whole_tiles(piece[1])), bf16) for piece in right[1:] * 2 + left * 2]
    logprobs, target = pl.pallas_call(
        functools.partial(kernel, n, tp_size, plane, width),
        out_shape=(
            jax.ShapeDtypeStruct((rows, width), bf16),
            jax.ShapeDtypeStruct((1, own_rows), f32),
        ),
        in_specs=[any_space, any_space, vmem, vmem],
        out_specs=(vmem, vmem),
        scratch_shapes=[
            pltpu.VMEM((rows, depth), bf16),
            pltpu.VMEM((block, depth), bf16),
            pltpu.VMEM((rows, depth), bf16),
            pltpu.VMEM((n, rows, widest), f32),
            pltpu.VMEM((CHUNKS, rc, whole_tiles(width)), f32),
            pltpu.VMEM((rows, LANES), jnp.int32),
            pltpu.VMEM((CHUNKS, 8, whole_tiles(rc + own_rows)), f32),
            pltpu.VMEM((CHUNKS, 8, rc), f32),
            pltpu.VMEM((n, CHUNKS, 8, rc), f32),
            pltpu.VMEM((CHUNKS, 8, rc), f32),
            pltpu.VMEM((CHUNKS, plane, 8, rc), f32),
            pltpu.VMEM((CHUNKS, 8, rc), f32),
            pltpu.VMEM((CHUNKS, n, 8, rc), f32),
            dma((2,)),
            dma((n, CHUNKS)),
            dma((n, CHUNKS)),
            dma((n, CHUNKS)),
            dma((n,)),
            dma((n,)),
            dma((CHUNKS, plane)),
            dma((CHUNKS, plane)),
            dma((CHUNKS, n)),
            dma((CHUNKS, n)),
        ] + travel,
        compiler_params=pltpu.CompilerParams(
            collective_id=0, has_side_effects=True, vmem_limit_bytes=52 * 1024 * 1024
        ),
        cost_estimate=pl.CostEstimate(
            flops=2 * rows * depth * block,
            bytes_accessed=2 * (rows * depth + depth * block + rows * width),
            transcendentals=rows * width,
        ),
    )(hidden_states, lm_head.T, norm_gain[None, :], target_ids)
    return logprobs, target.reshape(own_rows)


def solution(mesh):
    placed = (P(None, "dp"), P("dp"), P("dp", ("section", "tp")), P())
    return jax.shard_map(
        body,
        mesh=mesh,
        in_specs=placed,
        out_specs=(P(None, ("section", "tp", "dp")), P("dp")),
        check_vma=False,
    )
```

```python
import functools

import jax
import jax.numpy as jnp
from jax import lax
from jax.experimental import pallas as pl
from jax.experimental.pallas import tpu as pltpu
from jax.sharding import PartitionSpec as P

D = 8192

epsilon = 1e-06

MESH = pl.DeviceIdType.MESH
CHUNKS = 7
AHEAD = 3
LANES = 128
GRAIN = 8


def to_column(row):
    return jnp.broadcast_to(row, (LANES, row.shape[1])).T[:, :1]


def stack_rows(rows):
    place = lax.broadcasted_iota(jnp.int32, (8, rows[0].shape[1]), 0)
    result = jnp.zeros(place.shape, jnp.float32)
    for index, row in enumerate(rows):
        result = jnp.where(place == index, row, result)
    return result


def columns_to_rows(columns):
    place = lax.broadcasted_iota(jnp.int32, (columns[0].shape[0], LANES), 1)
    result = jnp.zeros(place.shape, jnp.float32)
    for index, column in enumerate(columns):
        result = jnp.where(place == index, column, result)
    return result.T[:8]


def merge(stats):
    tops, totals, picked = stats[:, 0:1], stats[:, 1:2], stats[:, 2:3]
    top = jnp.max(tops, axis=0)
    total = jnp.sum(totals * jnp.exp(tops - top[None]), axis=0)
    return top, total, jnp.sum(picked, axis=0)


def plan(n, width, block):
    origin = block - whole_tiles(block - width)
    starts = [(width * b - origin) // LANES * LANES for b in range(1, n)] + [block - origin]
    right = [None] + [(origin + lo, hi - lo) for lo, hi in zip(starts, starts[1:])]
    ends = [0] + [-(-width * (b + 1) // LANES) * LANES for b in range(n - 1)]
    left = [(lo, hi - lo) for lo, hi in zip(ends, ends[1:])]
    widest = max(piece[1] for piece in right[1:] + left)
    own = [(min(width * b // GRAIN * GRAIN, block - widest), widest) for b in range(n)]
    return right, left, own


def travel_order(n, at):
    going = [(at + n - 1 - b, "right", b) for b in range(n - 1, at, -1)]
    going += [(n - 1 - at + b, "left", b) for b in range(at)]
    return [entry[1:] for entry in sorted(going, key=lambda entry: entry[0])]


def whole_tiles(count):
    return -(-count // LANES) * LANES


def kernel(
    n, tp_size, plane, width,
    x_hbm, w_hbm, gain_ref, target_ref,
    out_ref, target_out_ref,
    x_buf, w_buf, xg, part, final, target_col, target_row,
    squares, all_squares, own_stats, plane_stats, own_merged, line_stats,
    load_sem, send_sem, left_sem, right_sem,
    sq_send, sq_recv, st_send, st_recv, ln_send, ln_recv,
    *travel,
):
    z = lax.axis_index("dp")
    me = lax.axis_index("section") * tp_size + lax.axis_index("tp")
    rc, widest = xg.shape[0] // CHUNKS, part.shape[2]
    right, left, own = plan(n, width, w_buf.shape[0])
    send_right, travel = (None,) + travel[:n - 1], travel[n - 1:]
    from_left, travel = (None,) + travel[:n - 1], travel[n - 1:]
    send_left, from_right = travel[:n - 1], travel[n - 1:]

    load_x = pltpu.make_async_copy(x_hbm, x_buf, load_sem.at[0])
    load_w = pltpu.make_async_copy(w_hbm, w_buf, load_sem.at[1])
    load_x.start()
    load_w.start()

    def plane_peer(step):
        q = lax.rem(me + step, plane)
        return q, {"section": q // tp_size, "tp": lax.rem(q, tp_size)}

    def line_peer(step):
        q = lax.rem(z + step, n)
        return q, {"dp": q}

    barrier = pltpu.get_barrier_semaphore()

    def greet(peer, step, carry):
        pl.semaphore_signal(barrier, inc=1, device_id=peer(step)[1], device_id_type=MESH)
        return carry

    lax.fori_loop(1, plane, functools.partial(greet, plane_peer), 0)
    lax.fori_loop(1, n, functools.partial(greet, line_peer), 0)

    target_col[...] = jnp.broadcast_to(
        target_ref[...].reshape(1, target_ref.shape[0]), (LANES, target_ref.shape[0])
    ).T
    load_x.wait()
    gain = gain_ref[...]

    def prepare(r, carry):
        x = x_buf[pl.ds(pl.multiple_of(r * rc, 16), rc), :].astype(jnp.float32)
        xg[pl.ds(pl.multiple_of(r * rc, 16), rc), :] = (x * gain).astype(jnp.bfloat16)
        squares[r] = columns_to_rows([jnp.sum(x * x, axis=1, keepdims=True)])
        return carry

    lax.fori_loop(0, CHUNKS, prepare, 0)
    pl.semaphore_wait(barrier, plane - 1 + n - 1)

    def squares_copy(step, arriving):
        q, where = line_peer(step)
        slot = q if arriving else z
        return pltpu.make_async_remote_copy(
            src_ref=squares, dst_ref=all_squares.at[slot],
            send_sem=sq_send.at[step], recv_sem=sq_recv.at[slot],
            device_id=where, device_id_type=MESH,
        )

    def stats_copy(r, step, arriving):
        q, where = plane_peer(step)
        slot = q if arriving else me
        return pltpu.make_async_remote_copy(
            src_ref=own_stats.at[r], dst_ref=plane_stats.at[r, slot],
            send_sem=st_send.at[r, step], recv_sem=st_recv.at[r, slot],
            device_id=where, device_id_type=MESH,
        )

    def line_copy(r, step, arriving):
        q, where = line_peer(step)
        slot = q if arriving else z
        return pltpu.make_async_remote_copy(
            src_ref=own_merged.at[r], dst_ref=line_stats.at[r, slot],
            send_sem=ln_send.at[r, step], recv_sem=ln_recv.at[r, slot],
            device_id=where, device_id_type=MESH,
        )

    def each(first, last, action):
        def step_body(step, carry):
            action(step)
            return carry
        lax.fori_loop(first, last, step_body, 0)

    each(1, n, lambda step: squares_copy(step, False).start())
    all_squares[z] = squares[...]
    load_w.wait()

    def right_copy(at, b, r):
        return pltpu.make_async_remote_copy(
            src_ref=send_right[b].at[r], dst_ref=from_left[b].at[r],
            send_sem=send_sem.at[b, r], recv_sem=left_sem.at[b, r],
            device_id={"dp": min(at + 1, n - 1)}, device_id_type=MESH,
        )

    def left_copy(at, b, r):
        return pltpu.make_async_remote_copy(
            src_ref=send_left[b].at[r], dst_ref=from_right[b].at[r],
            send_sem=send_sem.at[b, r], recv_sem=right_sem.at[b, r],
            device_id={"dp": max(at - 1, 0)}, device_id_type=MESH,
        )

    orders = [travel_order(n, at) for at in range(n)]

    def rows_of(r):
        return pl.ds(pl.multiple_of(r * rc, 16), rc)

    def start_own(at, k, r):
        way, b = orders[at][k]
        if way == "right":
            send_right[b][r] = part[k, rows_of(r), :right[b][1]].astype(jnp.bfloat16)
            right_copy(at, b, r).start()
        else:
            send_left[b][r] = part[k, rows_of(r), :left[b][1]].astype(jnp.bfloat16)
            left_copy(at, b, r).start()

    def multiply(k, carry):
        first = 0
        for at in range(n):
            pieces = [(right if way == "right" else left)[b] for way, b in orders[at]] + [own[at]]
            for index, piece in enumerate(pieces):
                first = jnp.where((z == at) & (k == index), piece[0], first)
        part[k] = lax.dot_general(
            xg[...], w_buf[pl.ds(pl.multiple_of(first, GRAIN), widest), :],
            (((1,), (1,)), ((), ())), preferred_element_type=jnp.float32,
        )
        for at in (0, n - 1):
            for index in range(n - 1):
                pl.when((z == at) & (k == index))(functools.partial(start_own, at, index, 0))
        return carry

    lax.fori_loop(0, n, multiply, 0)

    def shifted(parts, lead):
        lanes = jnp.concatenate([p.astype(jnp.float32) for p in parts], axis=1) if len(parts) > 1 else parts[0].astype(jnp.float32)
        if lead:
            lanes = pltpu.roll(lanes, lanes.shape[1] - lead, 1)
        return lanes[:, :final.shape[2]]

    def window(buffers, pieces, origin, at, r):
        lo, hi = width * at, width * (at + 1)
        first, parts = None, []
        for buffer, piece in zip(buffers, pieces):
            if piece is None or piece[0] + piece[1] <= lo or piece[0] >= hi:
                continue
            begin = max(lo - piece[0], 0) // LANES * LANES
            end = min(whole_tiles(hi - piece[0]), whole_tiles(piece[1]))
            if first is None:
                first = piece[0] + begin
            parts.append(buffer[r, :, begin:end])
        return shifted(parts, lo - first)

    def run(at):
        going = orders[at]
        end = at in (0, n - 1)

        def forward(r):
            for k, (way, b) in enumerate(going):
                if way == "right":
                    count = right[b][1]
                    right_copy(at, b, r).wait_recv()
                    send_right[b][r] = (
                        part[k, rows_of(r), :count] + from_left[b][r].astype(jnp.float32)
                    ).astype(jnp.bfloat16)
                    right_copy(at, b, r).start()
                else:
                    count = left[b][1]
                    left_copy(at, b, r).wait_recv()
                    send_left[b][r] = (
                        part[k, rows_of(r), :count] + from_right[b][r].astype(jnp.float32)
                    ).astype(jnp.bfloat16)
                    left_copy(at, b, r).start()

        def finish_sum(r):
            total = jnp.sum(all_squares[:, r], axis=0)[0:1]
            scale = to_column(lax.rsqrt(total / D + epsilon))
            logits = shifted([part[n - 1, rows_of(r)]], width * at - own[at][0])
            if at > 0:
                right_copy(at, at, r).wait_recv()
                logits += window(from_left, right, right[1][0], at, r)
            if at < n - 1:
                left_copy(at, at, r).wait_recv()
                logits += window(from_right, left, 0, at, r)
            logits *= scale
            final[r] = logits
            column = lax.broadcasted_iota(jnp.int32, logits.shape, 1)
            inside = column < width
            top = jnp.max(jnp.where(inside, logits, -jnp.inf), axis=1, keepdims=True)
            sum_exp = jnp.sum(jnp.where(inside, jnp.exp(logits - top), 0.0), axis=1, keepdims=True)
            wanted = target_col[pl.ds(pl.multiple_of(r * rc, 16), rc), 0:1] - (me * n + at) * width
            hit = inside & (column == wanted)
            picked = jnp.sum(jnp.where(hit, logits, 0.0), axis=1, keepdims=True)
            stats = columns_to_rows([top, sum_exp, picked])
            own_stats[r] = stats
            plane_stats[r, me] = stats
            each(1, plane, lambda step: stats_copy(r, step, False).start())

        def merge_plane(r):
            each(1, plane, lambda step: stats_copy(r, step, True).wait_recv())
            merged = stack_rows(merge(plane_stats[r]))
            own_merged[r] = merged
            line_stats[r, at] = merged
            each(1, n, lambda step: line_copy(r, step, False).start())

        def emit(r):
            each(1, n, lambda step: line_copy(r, step, True).wait_recv())
            top, total, picked = merge(line_stats[r])
            rest = jnp.log(total)
            target_row[r, :, :rc] = jnp.broadcast_to(picked - top - rest, (8, rc))
            logprobs = final[r] - to_column(top + rest)
            out_ref[pl.ds(pl.multiple_of(r * rc, 16), rc), :] = logprobs[:, :width].astype(jnp.bfloat16)

        def start_chunk(r):
            for k in range(n - 1):
                start_own(at, k, r)

        if end:
            for r in range(1, AHEAD):
                start_chunk(r)
        each(1, n, lambda step: squares_copy(step, True).wait_recv())

        def chunk(r, carry):
            if end:
                @pl.when(r + AHEAD < CHUNKS)
                def _():
                    start_chunk(r + AHEAD)
            else:
                forward(r)

            @pl.when(r >= 2)
            def _():
                merge_plane(r - 2)
            finish_sum(r)
            return carry

        def emit_step(r, carry):
            emit(r)
            return carry

        lax.fori_loop(0, CHUNKS, chunk, 0)
        merge_plane(CHUNKS - 2)
        lax.fori_loop(0, CHUNKS // 2, emit_step, 0)
        merge_plane(CHUNKS - 1)
        lax.fori_loop(CHUNKS // 2, CHUNKS, emit_step, 0)

        own_rows = target_out_ref.shape[1]
        lo = own_rows * at
        lanes = target_row.shape[2]
        place = lax.broadcasted_iota(jnp.int32, (8, lanes), 1) + lo
        row = jnp.zeros((8, lanes), jnp.float32)
        for c in range(lo // rc, (lo + own_rows - 1) // rc + 1):
            moved = pltpu.roll(target_row[c], (c * rc - lo) % lanes, 1)
            row = jnp.where((place >= c * rc) & (place < (c + 1) * rc), moved, row)
        target_out_ref[...] = row[0:1, :own_rows]

        for r in range(CHUNKS):
            for way, b in going:
                (right_copy if way == "right" else left_copy)(at, b, r).wait_send()

    for at in range(n):
        pl.when(z == at)(functools.partial(run, at))

    each(1, n, lambda step: squares_copy(step, False).wait_send())

    def drain(r, carry):
        each(1, plane, lambda step: stats_copy(r, step, False).wait_send())
        each(1, n, lambda step: line_copy(r, step, False).wait_send())
        return carry

    lax.fori_loop(0, CHUNKS, drain, 0)


def body(hidden_states, norm_gain, lm_head, target_ids):
    rows, depth = hidden_states.shape
    block = lm_head.shape[1]
    n, tp_size = lax.axis_size("dp"), lax.axis_size("tp")
    plane = lax.axis_size("section") * tp_size
    width = block // n
    right, left, own = plan(n, width, block)
    widest = max(whole_tiles(piece[1]) for piece in right[1:] + left + own)
    rc = rows // CHUNKS
    own_rows = rows // n
    f32, bf16 = jnp.float32, jnp.bfloat16
    any_space = pl.BlockSpec(memory_space=pl.ANY)
    vmem = pl.BlockSpec(memory_space=pltpu.VMEM)
    dma = pltpu.SemaphoreType.DMA
    travel = [pltpu.VMEM((CHUNKS, rc, whole_tiles(piece[1])), bf16) for piece in right[1:] * 2 + left * 2]
    logprobs, target = pl.pallas_call(
        functools.partial(kernel, n, tp_size, plane, width),
        out_shape=(
            jax.ShapeDtypeStruct((rows, width), bf16),
            jax.ShapeDtypeStruct((1, own_rows), f32),
        ),
        in_specs=[any_space, any_space, vmem, vmem],
        out_specs=(vmem, vmem),
        scratch_shapes=[
            pltpu.VMEM((rows, depth), bf16),
            pltpu.VMEM((block, depth), bf16),
            pltpu.VMEM((rows, depth), bf16),
            pltpu.VMEM((n, rows, widest), f32),
            pltpu.VMEM((CHUNKS, rc, whole_tiles(width)), f32),
            pltpu.VMEM((rows, LANES), jnp.int32),
            pltpu.VMEM((CHUNKS, 8, whole_tiles(rc + own_rows)), f32),
            pltpu.VMEM((CHUNKS, 8, rc), f32),
            pltpu.VMEM((n, CHUNKS, 8, rc), f32),
            pltpu.VMEM((CHUNKS, 8, rc), f32),
            pltpu.VMEM((CHUNKS, plane, 8, rc), f32),
            pltpu.VMEM((CHUNKS, 8, rc), f32),
            pltpu.VMEM((CHUNKS, n, 8, rc), f32),
            dma((2,)),
            dma((n, CHUNKS)),
            dma((n, CHUNKS)),
            dma((n, CHUNKS)),
            dma((n,)),
            dma((n,)),
            dma((CHUNKS, plane)),
            dma((CHUNKS, plane)),
            dma((CHUNKS, n)),
            dma((CHUNKS, n)),
        ] + travel,
        compiler_params=pltpu.CompilerParams(
            collective_id=0, has_side_effects=True, vmem_limit_bytes=52 * 1024 * 1024
        ),
        cost_estimate=pl.CostEstimate(
            flops=2 * rows * depth * block,
            bytes_accessed=2 * (rows * depth + depth * block + rows * width),
            transcendentals=rows * width,
        ),
    )(hidden_states, lm_head.T, norm_gain[None, :], target_ids)
    return logprobs, target.reshape(own_rows)


def solution(mesh):
    placed = (P(None, "dp"), P("dp"), P("dp", ("section", "tp")), P())
    return jax.shard_map(
        body,
        mesh=mesh,
        in_specs=placed,
        out_specs=(P(None, ("section", "tp", "dp")), P("dp")),
        check_vma=False,
    )
```

```python
import functools

import jax
import jax.numpy as jnp
from jax import lax
from jax.experimental import pallas as pl
from jax.experimental.pallas import tpu as pltpu
from jax.sharding import PartitionSpec as P

D = 8192

epsilon = 1e-06

MESH = pl.DeviceIdType.MESH
CHUNKS = 7
AHEAD = 2
LAG = 4
LANES = 128
GRAIN = 8


def to_column(row):
    return jnp.broadcast_to(row, (LANES, row.shape[1])).T[:, :1]


def stack_rows(rows):
    place = lax.broadcasted_iota(jnp.int32, (8, rows[0].shape[1]), 0)
    result = jnp.zeros(place.shape, jnp.float32)
    for index, row in enumerate(rows):
        result = jnp.where(place == index, row, result)
    return result


def columns_to_rows(columns):
    place = lax.broadcasted_iota(jnp.int32, (columns[0].shape[0], LANES), 1)
    result = jnp.zeros(place.shape, jnp.float32)
    for index, column in enumerate(columns):
        result = jnp.where(place == index, column, result)
    return result.T[:8]


def merge(stats):
    tops, totals, picked = stats[:, 0:1], stats[:, 1:2], stats[:, 2:3]
    top = jnp.max(tops, axis=0)
    total = jnp.sum(totals * jnp.exp(tops - top[None]), axis=0)
    return top, total, jnp.sum(picked, axis=0)


def plan(n, width, block):
    origin = block - whole_tiles(block - width)
    starts = [(width * b - origin) // LANES * LANES for b in range(1, n)] + [block - origin]
    right = [None] + [(origin + lo, hi - lo) for lo, hi in zip(starts, starts[1:])]
    ends = [0] + [-(-width * (b + 1) // LANES) * LANES for b in range(n - 1)]
    left = [(lo, hi - lo) for lo, hi in zip(ends, ends[1:])]
    widest = max(piece[1] for piece in right[1:] + left)
    own = [(min(width * b // GRAIN * GRAIN, block - widest), widest) for b in range(n)]
    return right, left, own


def travel_order(n, at):
    going = [(at + n - 1 - b, "right", b) for b in range(n - 1, at, -1)]
    going += [(n - 1 - at + b, "left", b) for b in range(at)]
    return [entry[1:] for entry in sorted(going, key=lambda entry: entry[0])]


def whole_tiles(count):
    return -(-count // LANES) * LANES


def kernel(
    n, tp_size, plane, width,
    x_hbm, w_hbm, gain_ref, target_ref,
    out_ref, target_out_ref,
    x_buf, w_buf, xg, part, final, target_col, target_row,
    squares, all_squares, own_stats, plane_stats, own_merged, line_stats,
    load_sem, send_sem, left_sem, right_sem,
    sq_send, sq_recv, st_send, st_recv, ln_send, ln_recv,
    *travel,
):
    z = lax.axis_index("dp")
    me = lax.axis_index("section") * tp_size + lax.axis_index("tp")
    rc, widest = xg.shape[0] // CHUNKS, part.shape[2]
    right, left, own = plan(n, width, w_buf.shape[0])
    send_right, travel = (None,) + travel[:n - 1], travel[n - 1:]
    from_left, travel = (None,) + travel[:n - 1], travel[n - 1:]
    send_left, from_right = travel[:n - 1], travel[n - 1:]

    load_x = pltpu.make_async_copy(x_hbm, x_buf, load_sem.at[0])
    load_w = pltpu.make_async_copy(w_hbm, w_buf, load_sem.at[1])
    load_x.start()
    load_w.start()

    def plane_peer(step):
        q = lax.rem(me + step, plane)
        return q, {"section": q // tp_size, "tp": lax.rem(q, tp_size)}

    def line_peer(step):
        q = lax.rem(z + step, n)
        return q, {"dp": q}

    barrier = pltpu.get_barrier_semaphore()

    def greet(peer, step, carry):
        pl.semaphore_signal(barrier, inc=1, device_id=peer(step)[1], device_id_type=MESH)
        return carry

    lax.fori_loop(1, plane, functools.partial(greet, plane_peer), 0)
    lax.fori_loop(1, n, functools.partial(greet, line_peer), 0)

    target_col[...] = jnp.broadcast_to(
        target_ref[...].reshape(1, target_ref.shape[0]), (LANES, target_ref.shape[0])
    ).T
    load_x.wait()
    gain = gain_ref[...]

    def prepare(r, carry):
        x = x_buf[pl.ds(pl.multiple_of(r * rc, 16), rc), :].astype(jnp.float32)
        xg[pl.ds(pl.multiple_of(r * rc, 16), rc), :] = (x * gain).astype(jnp.bfloat16)
        squares[r] = columns_to_rows([jnp.sum(x * x, axis=1, keepdims=True)])
        return carry

    lax.fori_loop(0, CHUNKS, prepare, 0)
    pl.semaphore_wait(barrier, plane - 1 + n - 1)

    def squares_copy(step, arriving):
        q, where = line_peer(step)
        slot = q if arriving else z
        return pltpu.make_async_remote_copy(
            src_ref=squares, dst_ref=all_squares.at[slot],
            send_sem=sq_send.at[step], recv_sem=sq_recv.at[slot],
            device_id=where, device_id_type=MESH,
        )

    def stats_copy(r, step, arriving):
        q, where = plane_peer(step)
        slot = q if arriving else me
        return pltpu.make_async_remote_copy(
            src_ref=own_stats.at[r], dst_ref=plane_stats.at[r, slot],
            send_sem=st_send.at[r, step], recv_sem=st_recv.at[r, slot],
            device_id=where, device_id_type=MESH,
        )

    def line_copy(r, step, arriving):
        q, where = line_peer(step)
        slot = q if arriving else z
        return pltpu.make_async_remote_copy(
            src_ref=own_merged.at[r], dst_ref=line_stats.at[r, slot],
            send_sem=ln_send.at[r, step], recv_sem=ln_recv.at[r, slot],
            device_id=where, device_id_type=MESH,
        )

    def each(first, last, action):
        def step_body(step, carry):
            action(step)
            return carry
        lax.fori_loop(first, last, step_body, 0)

    each(1, n, lambda step: squares_copy(step, False).start())
    all_squares[z] = squares[...]
    load_w.wait()

    def right_copy(at, b, r):
        return pltpu.make_async_remote_copy(
            src_ref=send_right[b].at[r], dst_ref=from_left[b].at[r],
            send_sem=send_sem.at[b, r], recv_sem=left_sem.at[b, r],
            device_id={"dp": min(at + 1, n - 1)}, device_id_type=MESH,
        )

    def left_copy(at, b, r):
        return pltpu.make_async_remote_copy(
            src_ref=send_left[b].at[r], dst_ref=from_right[b].at[r],
            send_sem=send_sem.at[b, r], recv_sem=right_sem.at[b, r],
            device_id={"dp": max(at - 1, 0)}, device_id_type=MESH,
        )

    orders = [travel_order(n, at) for at in range(n)]

    def rows_of(r):
        return pl.ds(pl.multiple_of(r * rc, 16), rc)

    def start_own(at, k, r):
        way, b = orders[at][k]
        if way == "right":
            send_right[b][r] = part[k, rows_of(r), :right[b][1]].astype(jnp.bfloat16)
            right_copy(at, b, r).start()
        else:
            send_left[b][r] = part[k, rows_of(r), :left[b][1]].astype(jnp.bfloat16)
            left_copy(at, b, r).start()

    def multiply(k, carry):
        first = 0
        for at in range(n):
            pieces = [(right if way == "right" else left)[b] for way, b in orders[at]] + [own[at]]
            for index, piece in enumerate(pieces):
                first = jnp.where((z == at) & (k == index), piece[0], first)
        part[k] = lax.dot_general(
            xg[...], w_buf[pl.ds(pl.multiple_of(first, GRAIN), widest), :],
            (((1,), (1,)), ((), ())), preferred_element_type=jnp.float32,
        )
        for at in (0, n - 1):
            for index in range(n - 1):
                for r in range(AHEAD):
                    pl.when((z == at) & (k == index))(functools.partial(start_own, at, index, r))
        return carry

    lax.fori_loop(0, n, multiply, 0)

    def shifted(parts, lead):
        lanes = jnp.concatenate([p.astype(jnp.float32) for p in parts], axis=1) if len(parts) > 1 else parts[0].astype(jnp.float32)
        if lead:
            lanes = pltpu.roll(lanes, lanes.shape[1] - lead, 1)
        return lanes[:, :final.shape[2]]

    def window(buffers, pieces, origin, at, r):
        lo, hi = width * at, width * (at + 1)
        first, parts = None, []
        for buffer, piece in zip(buffers, pieces):
            if piece is None or piece[0] + piece[1] <= lo or piece[0] >= hi:
                continue
            begin = max(lo - piece[0], 0) // LANES * LANES
            end = min(whole_tiles(hi - piece[0]), whole_tiles(piece[1]))
            if first is None:
                first = piece[0] + begin
            parts.append(buffer[r, :, begin:end])
        return shifted(parts, lo - first)

    def run(at):
        going = orders[at]
        end = at in (0, n - 1)

        def forward(r):
            for k, (way, b) in enumerate(going):
                if way == "right":
                    count = right[b][1]
                    right_copy(at, b, r).wait_recv()
                    send_right[b][r] = (
                        part[k, rows_of(r), :count] + from_left[b][r].astype(jnp.float32)
                    ).astype(jnp.bfloat16)
                    right_copy(at, b, r).start()
                else:
                    count = left[b][1]
                    left_copy(at, b, r).wait_recv()
                    send_left[b][r] = (
                        part[k, rows_of(r), :count] + from_right[b][r].astype(jnp.float32)
                    ).astype(jnp.bfloat16)
                    left_copy(at, b, r).start()

        def finish_sum(r):
            total = jnp.sum(all_squares[:, r], axis=0)[0:1]
            scale = to_column(lax.rsqrt(total / D + epsilon))
            logits = shifted([part[n - 1, rows_of(r)]], width * at - own[at][0])
            if at > 0:
                right_copy(at, at, r).wait_recv()
                logits += window(from_left, right, right[1][0], at, r)
            if at < n - 1:
                left_copy(at, at, r).wait_recv()
                logits += window(from_right, left, 0, at, r)
            logits *= scale
            final[r] = logits
            column = lax.broadcasted_iota(jnp.int32, logits.shape, 1)
            inside = column < width
            top = jnp.max(jnp.where(inside, logits, -jnp.inf), axis=1, keepdims=True)
            sum_exp = jnp.sum(jnp.where(inside, jnp.exp(logits - top), 0.0), axis=1, keepdims=True)
            wanted = target_col[pl.ds(pl.multiple_of(r * rc, 16), rc), 0:1] - (me * n + at) * width
            hit = inside & (column == wanted)
            picked = jnp.sum(jnp.where(hit, logits, 0.0), axis=1, keepdims=True)
            stats = columns_to_rows([top, sum_exp, picked])
            own_stats[r] = stats
            plane_stats[r, me] = stats
            each(1, plane, lambda step: stats_copy(r, step, False).start())

        def merge_plane(r):
            each(1, plane, lambda step: stats_copy(r, step, True).wait_recv())
            merged = stack_rows(merge(plane_stats[r]))
            own_merged[r] = merged
            line_stats[r, at] = merged
            each(1, n, lambda step: line_copy(r, step, False).start())

        def emit(r):
            each(1, n, lambda step: line_copy(r, step, True).wait_recv())
            top, total, picked = merge(line_stats[r])
            rest = jnp.log(total)
            target_row[r, :, :rc] = jnp.broadcast_to(picked - top - rest, (8, rc))
            logprobs = final[r] - to_column(top + rest)
            out_ref[pl.ds(pl.multiple_of(r * rc, 16), rc), :] = logprobs[:, :width].astype(jnp.bfloat16)

        def start_chunk(r):
            for k in range(n - 1):
                start_own(at, k, r)

        each(1, n, lambda step: squares_copy(step, True).wait_recv())

        def chunk(r, carry):
            if not end:
                forward(r)

            @pl.when(r >= 1)
            def _():
                merge_plane(r - 1)

            if end:
                @pl.when(r + AHEAD < CHUNKS)
                def _():
                    start_chunk(r + AHEAD)

            @pl.when(r >= LAG)
            def _():
                emit(r - LAG)
            finish_sum(r)
            return carry

        lax.fori_loop(0, CHUNKS, chunk, 0)
        emit(CHUNKS - LAG)
        merge_plane(CHUNKS - 1)

        def emit_step(r, carry):
            emit(r)
            return carry

        lax.fori_loop(CHUNKS - LAG + 1, CHUNKS, emit_step, 0)

        own_rows = target_out_ref.shape[1]
        lo = own_rows * at
        lanes = target_row.shape[2]
        place = lax.broadcasted_iota(jnp.int32, (8, lanes), 1) + lo
        row = jnp.zeros((8, lanes), jnp.float32)
        for c in range(lo // rc, (lo + own_rows - 1) // rc + 1):
            moved = pltpu.roll(target_row[c], (c * rc - lo) % lanes, 1)
            row = jnp.where((place >= c * rc) & (place < (c + 1) * rc), moved, row)
        target_out_ref[...] = row[0:1, :own_rows]

        for r in range(CHUNKS):
            for way, b in going:
                (right_copy if way == "right" else left_copy)(at, b, r).wait_send()

    for at in range(n):
        pl.when(z == at)(functools.partial(run, at))

    each(1, n, lambda step: squares_copy(step, False).wait_send())

    def drain(r, carry):
        each(1, plane, lambda step: stats_copy(r, step, False).wait_send())
        each(1, n, lambda step: line_copy(r, step, False).wait_send())
        return carry

    lax.fori_loop(0, CHUNKS, drain, 0)


def body(hidden_states, norm_gain, lm_head, target_ids):
    rows, depth = hidden_states.shape
    block = lm_head.shape[1]
    n, tp_size = lax.axis_size("dp"), lax.axis_size("tp")
    plane = lax.axis_size("section") * tp_size
    width = block // n
    right, left, own = plan(n, width, block)
    widest = max(whole_tiles(piece[1]) for piece in right[1:] + left + own)
    rc = rows // CHUNKS
    own_rows = rows // n
    f32, bf16 = jnp.float32, jnp.bfloat16
    any_space = pl.BlockSpec(memory_space=pl.ANY)
    vmem = pl.BlockSpec(memory_space=pltpu.VMEM)
    dma = pltpu.SemaphoreType.DMA
    travel = [pltpu.VMEM((CHUNKS, rc, whole_tiles(piece[1])), bf16) for piece in right[1:] * 2 + left * 2]
    logprobs, target = pl.pallas_call(
        functools.partial(kernel, n, tp_size, plane, width),
        out_shape=(
            jax.ShapeDtypeStruct((rows, width), bf16),
            jax.ShapeDtypeStruct((1, own_rows), f32),
        ),
        in_specs=[any_space, any_space, vmem, vmem],
        out_specs=(vmem, vmem),
        scratch_shapes=[
            pltpu.VMEM((rows, depth), bf16),
            pltpu.VMEM((block, depth), bf16),
            pltpu.VMEM((rows, depth), bf16),
            pltpu.VMEM((n, rows, widest), f32),
            pltpu.VMEM((CHUNKS, rc, whole_tiles(width)), f32),
            pltpu.VMEM((rows, LANES), jnp.int32),
            pltpu.VMEM((CHUNKS, 8, whole_tiles(rc + own_rows)), f32),
            pltpu.VMEM((CHUNKS, 8, rc), f32),
            pltpu.VMEM((n, CHUNKS, 8, rc), f32),
            pltpu.VMEM((CHUNKS, 8, rc), f32),
            pltpu.VMEM((CHUNKS, plane, 8, rc), f32),
            pltpu.VMEM((CHUNKS, 8, rc), f32),
            pltpu.VMEM((CHUNKS, n, 8, rc), f32),
            dma((2,)),
            dma((n, CHUNKS)),
            dma((n, CHUNKS)),
            dma((n, CHUNKS)),
            dma((n,)),
            dma((n,)),
            dma((CHUNKS, plane)),
            dma((CHUNKS, plane)),
            dma((CHUNKS, n)),
            dma((CHUNKS, n)),
        ] + travel,
        compiler_params=pltpu.CompilerParams(
            collective_id=0, has_side_effects=True, vmem_limit_bytes=52 * 1024 * 1024
        ),
        cost_estimate=pl.CostEstimate(
            flops=2 * rows * depth * block,
            bytes_accessed=2 * (rows * depth + depth * block + rows * width),
            transcendentals=rows * width,
        ),
    )(hidden_states, lm_head.T, norm_gain[None, :], target_ids)
    return logprobs, target.reshape(own_rows)


def solution(mesh):
    placed = (P(None, "dp"), P("dp"), P("dp", ("section", "tp")), P())
    return jax.shard_map(
        body,
        mesh=mesh,
        in_specs=placed,
        out_specs=(P(None, ("section", "tp", "dp")), P("dp")),
        check_vma=False,
    )
```

```python
import functools

import jax
import jax.numpy as jnp
from jax import lax
from jax.experimental import pallas as pl
from jax.experimental.pallas import tpu as pltpu
from jax.sharding import PartitionSpec as P

D = 8192

epsilon = 1e-06

MESH = pl.DeviceIdType.MESH
CHUNKS = 3
LANES = 128
GRAIN = 8


def to_column(row):
    return jnp.broadcast_to(row, (LANES, row.shape[1])).T[:, :1]


def stack_rows(rows):
    place = lax.broadcasted_iota(jnp.int32, (8, rows[0].shape[1]), 0)
    result = jnp.zeros(place.shape, jnp.float32)
    for index, row in enumerate(rows):
        result = jnp.where(place == index, row, result)
    return result


def columns_to_rows(columns):
    place = lax.broadcasted_iota(jnp.int32, (columns[0].shape[0], LANES), 1)
    result = jnp.zeros(place.shape, jnp.float32)
    for index, column in enumerate(columns):
        result = jnp.where(place == index, column, result)
    return result.T[:8]


def merge(stats):
    tops, totals, picked = stats[:, 0:1], stats[:, 1:2], stats[:, 2:3]
    top = jnp.max(tops, axis=0)
    total = jnp.sum(totals * jnp.exp(tops - top[None]), axis=0)
    return top, total, jnp.sum(picked, axis=0)


def plan(n, width, block):
    origin = block - whole_tiles(block - width)
    starts = [(width * b - origin) // LANES * LANES for b in range(1, n)] + [block - origin]
    right = [None] + [(origin + lo, hi - lo) for lo, hi in zip(starts, starts[1:])]
    ends = [0] + [-(-width * (b + 1) // LANES) * LANES for b in range(n - 1)]
    left = [(lo, hi - lo) for lo, hi in zip(ends, ends[1:])]
    widest = max(piece[1] for piece in right[1:] + left)
    own = [(min(width * b // GRAIN * GRAIN, block - widest), widest) for b in range(n)]
    return right, left, own


def travel_order(n, at):
    going = [(at + n - 1 - b, "right", b) for b in range(n - 1, at, -1)]
    going += [(n - 1 - at + b, "left", b) for b in range(at)]
    return [entry[1:] for entry in sorted(going, key=lambda entry: entry[0])]


def whole_tiles(count):
    return -(-count // LANES) * LANES


def kernel(
    n, tp_size, plane, width,
    x_hbm, w_hbm, gain_ref, target_ref,
    out_ref, target_out_ref,
    x_buf, w_buf, xg, part, final, target_col, target_row,
    squares, all_squares, own_stats, plane_stats, own_merged, line_stats,
    load_sem, send_sem, left_sem, right_sem,
    sq_send, sq_recv, st_send, st_recv, ln_send, ln_recv,
    *travel,
):
    z = lax.axis_index("dp")
    me = lax.axis_index("section") * tp_size + lax.axis_index("tp")
    rc, widest = xg.shape[0] // CHUNKS, part.shape[2]
    right, left, own = plan(n, width, w_buf.shape[0])
    send_right, travel = (None,) + travel[:n - 1], travel[n - 1:]
    from_left, travel = (None,) + travel[:n - 1], travel[n - 1:]
    send_left, from_right = travel[:n - 1], travel[n - 1:]

    load_x = pltpu.make_async_copy(x_hbm, x_buf, load_sem.at[0])
    load_w = pltpu.make_async_copy(w_hbm, w_buf, load_sem.at[1])
    load_x.start()
    load_w.start()

    def plane_peer(step):
        q = lax.rem(me + step, plane)
        return q, {"section": q // tp_size, "tp": lax.rem(q, tp_size)}

    def line_peer(step):
        q = lax.rem(z + step, n)
        return q, {"dp": q}

    barrier = pltpu.get_barrier_semaphore()

    def greet(peer, step, carry):
        pl.semaphore_signal(barrier, inc=1, device_id=peer(step)[1], device_id_type=MESH)
        return carry

    lax.fori_loop(1, plane, functools.partial(greet, plane_peer), 0)
    lax.fori_loop(1, n, functools.partial(greet, line_peer), 0)

    target_col[...] = jnp.broadcast_to(
        target_ref[...].reshape(1, target_ref.shape[0]), (LANES, target_ref.shape[0])
    ).T
    load_x.wait()
    gain = gain_ref[...]

    def prepare(r, carry):
        x = x_buf[pl.ds(pl.multiple_of(r * rc, 16), rc), :].astype(jnp.float32)
        xg[pl.ds(pl.multiple_of(r * rc, 16), rc), :] = (x * gain).astype(jnp.bfloat16)
        squares[r] = columns_to_rows([jnp.sum(x * x, axis=1, keepdims=True)])
        return carry

    lax.fori_loop(0, CHUNKS, prepare, 0)
    pl.semaphore_wait(barrier, plane - 1 + n - 1)

    def squares_copy(step, arriving):
        q, where = line_peer(step)
        slot = q if arriving else z
        return pltpu.make_async_remote_copy(
            src_ref=squares, dst_ref=all_squares.at[slot],
            send_sem=sq_send.at[step], recv_sem=sq_recv.at[slot],
            device_id=where, device_id_type=MESH,
        )

    def stats_copy(r, step, arriving):
        q, where = plane_peer(step)
        slot = q if arriving else me
        return pltpu.make_async_remote_copy(
            src_ref=own_stats.at[r], dst_ref=plane_stats.at[r, slot],
            send_sem=st_send.at[r, step], recv_sem=st_recv.at[r, slot],
            device_id=where, device_id_type=MESH,
        )

    def line_copy(r, step, arriving):
        q, where = line_peer(step)
        slot = q if arriving else z
        return pltpu.make_async_remote_copy(
            src_ref=own_merged.at[r], dst_ref=line_stats.at[r, slot],
            send_sem=ln_send.at[r, step], recv_sem=ln_recv.at[r, slot],
            device_id=where, device_id_type=MESH,
        )

    def each(first, last, action):
        def step_body(step, carry):
            action(step)
            return carry
        lax.fori_loop(first, last, step_body, 0)

    each(1, n, lambda step: squares_copy(step, False).start())
    all_squares[z] = squares[...]
    load_w.wait()

    def right_copy(at, b, r):
        return pltpu.make_async_remote_copy(
            src_ref=send_right[b].at[r], dst_ref=from_left[b].at[r],
            send_sem=send_sem.at[b, r], recv_sem=left_sem.at[b, r],
            device_id={"dp": min(at + 1, n - 1)}, device_id_type=MESH,
        )

    def left_copy(at, b, r):
        return pltpu.make_async_remote_copy(
            src_ref=send_left[b].at[r], dst_ref=from_right[b].at[r],
            send_sem=send_sem.at[b, r], recv_sem=right_sem.at[b, r],
            device_id={"dp": max(at - 1, 0)}, device_id_type=MESH,
        )

    orders = [travel_order(n, at) for at in range(n)]

    def rows_of(r):
        return pl.ds(pl.multiple_of(r * rc, 16), rc)

    def start_own(at, k, r):
        way, b = orders[at][k]
        if way == "right":
            send_right[b][r] = part[k, rows_of(r), :right[b][1]].astype(jnp.bfloat16)
            right_copy(at, b, r).start()
        else:
            send_left[b][r] = part[k, rows_of(r), :left[b][1]].astype(jnp.bfloat16)
            left_copy(at, b, r).start()

    def multiply(r, k, carry):
        first = 0
        for at in range(n):
            pieces = [(right if way == "right" else left)[b] for way, b in orders[at]] + [own[at]]
            for index, piece in enumerate(pieces):
                first = jnp.where((z == at) & (k == index), piece[0], first)
        part[k, rows_of(r), :] = lax.dot_general(
            xg[rows_of(r), :], w_buf[pl.ds(pl.multiple_of(first, GRAIN), widest), :],
            (((1,), (1,)), ((), ())), preferred_element_type=jnp.float32,
        )
        for at in (0, n - 1):
            for index in range(n - 1):
                pl.when((z == at) & (k == index))(functools.partial(start_own, at, index, r))
        return carry

    def shifted(parts, lead):
        lanes = jnp.concatenate([p.astype(jnp.float32) for p in parts], axis=1) if len(parts) > 1 else parts[0].astype(jnp.float32)
        if lead:
            lanes = pltpu.roll(lanes, lanes.shape[1] - lead, 1)
        return lanes[:, :final.shape[2]]

    def window(buffers, pieces, origin, at, r):
        lo, hi = width * at, width * (at + 1)
        first, parts = None, []
        for buffer, piece in zip(buffers, pieces):
            if piece is None or piece[0] + piece[1] <= lo or piece[0] >= hi:
                continue
            begin = max(lo - piece[0], 0) // LANES * LANES
            end = min(whole_tiles(hi - piece[0]), whole_tiles(piece[1]))
            if first is None:
                first = piece[0] + begin
            parts.append(buffer[r, :, begin:end])
        return shifted(parts, lo - first)

    def run(at, stage, stage_r):
        going = orders[at]
        end = at in (0, n - 1)

        def forward(r):
            for k, (way, b) in enumerate(going):
                if way == "right":
                    count = right[b][1]
                    right_copy(at, b, r).wait_recv()
                    send_right[b][r] = (
                        part[k, rows_of(r), :count] + from_left[b][r].astype(jnp.float32)
                    ).astype(jnp.bfloat16)
                    right_copy(at, b, r).start()
                else:
                    count = left[b][1]
                    left_copy(at, b, r).wait_recv()
                    send_left[b][r] = (
                        part[k, rows_of(r), :count] + from_right[b][r].astype(jnp.float32)
                    ).astype(jnp.bfloat16)
                    left_copy(at, b, r).start()

        def finish_sum(r):
            total = jnp.sum(all_squares[:, r], axis=0)[0:1]
            scale = to_column(lax.rsqrt(total / D + epsilon))
            logits = shifted([part[n - 1, rows_of(r)]], width * at - own[at][0])
            if at > 0:
                right_copy(at, at, r).wait_recv()
                logits += window(from_left, right, right[1][0], at, r)
            if at < n - 1:
                left_copy(at, at, r).wait_recv()
                logits += window(from_right, left, 0, at, r)
            logits *= scale
            final[r] = logits
            column = lax.broadcasted_iota(jnp.int32, logits.shape, 1)
            inside = column < width
            top = jnp.max(jnp.where(inside, logits, -jnp.inf), axis=1, keepdims=True)
            sum_exp = jnp.sum(jnp.where(inside, jnp.exp(logits - top), 0.0), axis=1, keepdims=True)
            wanted = target_col[pl.ds(pl.multiple_of(r * rc, 16), rc), 0:1] - (me * n + at) * width
            hit = inside & (column == wanted)
            picked = jnp.sum(jnp.where(hit, logits, 0.0), axis=1, keepdims=True)
            stats = columns_to_rows([top, sum_exp, picked])
            own_stats[r] = stats
            plane_stats[r, me] = stats
            each(1, plane, lambda step: stats_copy(r, step, False).start())

        def merge_plane(r):
            each(1, plane, lambda step: stats_copy(r, step, True).wait_recv())
            merged = stack_rows(merge(plane_stats[r]))
            own_merged[r] = merged
            line_stats[r, at] = merged
            each(1, n, lambda step: line_copy(r, step, False).start())

        def emit(r):
            each(1, n, lambda step: line_copy(r, step, True).wait_recv())
            top, total, picked = merge(line_stats[r])
            rest = jnp.log(total)
            target_row[r, :, :rc] = jnp.broadcast_to(picked - top - rest, (8, rc))
            logprobs = final[r] - to_column(top + rest)
            out_ref[pl.ds(pl.multiple_of(r * rc, 16), rc), :] = logprobs[:, :width].astype(jnp.bfloat16)

        if stage == "before":
            if not end:
                forward(stage_r)
            else:
                pl.when(stage_r >= 1)(lambda: merge_plane(stage_r - 1))
            return
        if stage == "after":
            if not end:
                pl.when(stage_r >= 1)(lambda: merge_plane(stage_r - 1))
            finish_sum(stage_r)
            return

        emit(0)
        merge_plane(CHUNKS - 1)

        def emit_step(r, carry):
            emit(r)
            return carry

        lax.fori_loop(1, CHUNKS, emit_step, 0)

        own_rows = target_out_ref.shape[1]
        lo = own_rows * at
        lanes = target_row.shape[2]
        place = lax.broadcasted_iota(jnp.int32, (8, lanes), 1) + lo
        row = jnp.zeros((8, lanes), jnp.float32)
        for c in range(lo // rc, (lo + own_rows - 1) // rc + 1):
            moved = pltpu.roll(target_row[c], (c * rc - lo) % lanes, 1)
            row = jnp.where((place >= c * rc) & (place < (c + 1) * rc), moved, row)
        target_out_ref[...] = row[0:1, :own_rows]

        for r in range(CHUNKS):
            for way, b in going:
                (right_copy if way == "right" else left_copy)(at, b, r).wait_send()

    def run_here(stage, r):
        for at in range(n):
            pl.when(z == at)(functools.partial(run, at, stage, r))

    def chunk(t, carry):
        pl.when(t >= 1)(lambda: run_here("before", t - 1))

        @pl.when(t < CHUNKS)
        def _():
            lax.fori_loop(0, n, functools.partial(multiply, t), 0)

        @pl.when(t == 0)
        def _():
            each(1, n, lambda step: squares_copy(step, True).wait_recv())

        pl.when(t >= 1)(lambda: run_here("after", t - 1))
        return carry

    lax.fori_loop(0, CHUNKS + 1, chunk, 0)
    run_here("last", 0)

    each(1, n, lambda step: squares_copy(step, False).wait_send())

    def drain(r, carry):
        each(1, plane, lambda step: stats_copy(r, step, False).wait_send())
        each(1, n, lambda step: line_copy(r, step, False).wait_send())
        return carry

    lax.fori_loop(0, CHUNKS, drain, 0)


def body(hidden_states, norm_gain, lm_head, target_ids):
    rows, depth = hidden_states.shape
    block = lm_head.shape[1]
    n, tp_size = lax.axis_size("dp"), lax.axis_size("tp")
    plane = lax.axis_size("section") * tp_size
    width = block // n
    right, left, own = plan(n, width, block)
    widest = max(whole_tiles(piece[1]) for piece in right[1:] + left + own)
    rc = rows // CHUNKS
    own_rows = rows // n
    f32, bf16 = jnp.float32, jnp.bfloat16
    any_space = pl.BlockSpec(memory_space=pl.ANY)
    vmem = pl.BlockSpec(memory_space=pltpu.VMEM)
    dma = pltpu.SemaphoreType.DMA
    travel = [pltpu.VMEM((CHUNKS, rc, whole_tiles(piece[1])), bf16) for piece in right[1:] * 2 + left * 2]
    logprobs, target = pl.pallas_call(
        functools.partial(kernel, n, tp_size, plane, width),
        out_shape=(
            jax.ShapeDtypeStruct((rows, width), bf16),
            jax.ShapeDtypeStruct((1, own_rows), f32),
        ),
        in_specs=[any_space, any_space, vmem, vmem],
        out_specs=(vmem, vmem),
        scratch_shapes=[
            pltpu.VMEM((rows, depth), bf16),
            pltpu.VMEM((block, depth), bf16),
            pltpu.VMEM((rows, depth), bf16),
            pltpu.VMEM((n, rows, widest), f32),
            pltpu.VMEM((CHUNKS, rc, whole_tiles(width)), f32),
            pltpu.VMEM((rows, LANES), jnp.int32),
            pltpu.VMEM((CHUNKS, 8, whole_tiles(rc + own_rows)), f32),
            pltpu.VMEM((CHUNKS, 8, rc), f32),
            pltpu.VMEM((n, CHUNKS, 8, rc), f32),
            pltpu.VMEM((CHUNKS, 8, rc), f32),
            pltpu.VMEM((CHUNKS, plane, 8, rc), f32),
            pltpu.VMEM((CHUNKS, 8, rc), f32),
            pltpu.VMEM((CHUNKS, n, 8, rc), f32),
            dma((2,)),
            dma((n, CHUNKS)),
            dma((n, CHUNKS)),
            dma((n, CHUNKS)),
            dma((n,)),
            dma((n,)),
            dma((CHUNKS, plane)),
            dma((CHUNKS, plane)),
            dma((CHUNKS, n)),
            dma((CHUNKS, n)),
        ] + travel,
        compiler_params=pltpu.CompilerParams(
            collective_id=0, has_side_effects=True, vmem_limit_bytes=52 * 1024 * 1024
        ),
        cost_estimate=pl.CostEstimate(
            flops=2 * rows * depth * block,
            bytes_accessed=2 * (rows * depth + depth * block + rows * width),
            transcendentals=rows * width,
        ),
    )(hidden_states, lm_head.T, norm_gain[None, :], target_ids)
    return logprobs, target.reshape(own_rows)


def solution(mesh):
    placed = (P(None, "dp"), P("dp"), P("dp", ("section", "tp")), P())
    return jax.shard_map(
        body,
        mesh=mesh,
        in_specs=placed,
        out_specs=(P(None, ("section", "tp", "dp")), P("dp")),
        check_vma=False,
    )
```
